32 devices in a mesh: slab: 4 (over y, x), member: 8 (over z, core).
Axes of the slice: x: 2, y: 2, z: 4, core: 2. Of those that a mesh axis runs over, the one named last changes fastest.
Arguments:
- initial: float32 [64, 512, 1024], P('member', 'slab'), may hold values from -6 to 6
- stencil_numbers: float32 [3, 512, 1024], P(None, 'slab'), may hold values from -0.25 to 0.25, as said below
- innovations: float32 [64, 131072], P(None, ('slab', 'member')), may hold values from -6 to 6
- obs_prec: float32 [131072], P(('slab', 'member')), may hold values from 0.05 to 0.5
- obs_cell: int32 [4096, 32], P(('slab', 'member')), may hold values from 0 to 127
- band_idx: int32 [4096, 9], P(('slab', 'member')), may hold values from 0 to 4095, as said below
Outputs:
- analysis: float32 [64, 512, 1024], P('member', 'slab')
The draws below stay inside these ranges and needn't reach their ends.
Inputs may be any that keep to these rules, and one draw needn't show every extreme that they name: stencil_numbers[0] lies in 0.08 to 0.2; stencil_numbers[1] and stencil_numbers[2] lie in -0.25 to 0.25. `band_idx`: row b holds 9 distinct block indices j with |j - b| <= 8.
All inputs are finite; a program needn't handle non-finite values.
Results may differ from the reference program's by a relative error of at most 0.00011.
Values sent between devices are 32-bit elements; how exact they have to be, the bound alone decides.
No kernel may reach another device: no remote copies, remote signals or barrier semaphores. Data moves between devices by JAX's collectives and lax.ppermute only.
A program may use at most 128 MiB of HBM per device.

```python
import math
import jax
import jax.numpy as jnp
from jax import lax

LON = 1024
MEM_DEV = 8
STEPS = 4
OB = 32
R = 8
BAND = 9
NLAT = 512
REALIZATIONS = 64
TILE_TOTAL = 4096
NOBS = 131072
N_MEMBER = 8


def draw_stencil_numbers(key, part):
    key_diff, key_flow = jax.random.split(key)
    diffusion = jax.random.uniform(key_diff, (1, NLAT, LON), jnp.float32, 0.08, 0.2)
    flows = jax.random.uniform(key_flow, (2, NLAT, LON), jnp.float32, -0.25, 0.25)
    return jnp.concatenate([diffusion, flows], axis=0)


def draw_band_idx(key, part):
    width = 2 * R + 1
    offsets = jnp.arange(width, dtype=jnp.int32) - R
    blocks = jnp.arange(TILE_TOTAL, dtype=jnp.int32)[:, None] + offsets[None, :]
    is_valid = (blocks >= 0) & (blocks < TILE_TOTAL)
    scores = jax.random.randint(key, (TILE_TOTAL, width), 0, 1000, dtype=jnp.int32) * width + jnp.arange(width, dtype=jnp.int32)[None, :]
    scores = jnp.where(is_valid, scores + 1, -1)
    best_scores, positions = lax.top_k(scores, BAND)
    return jnp.take_along_axis(blocks, positions, axis=1).astype(jnp.int32)


def touch_ends(array, own_key, least, high):
    spot = [jax.random.randint(jax.random.fold_in(own_key, axis), (), 0, length) for axis, length in enumerate(array.shape)]
    main_axis = array.shape.index(max(array.shape))
    next_to = spot[:main_axis] + [(spot[main_axis] + 1) % array.shape[main_axis]] + spot[main_axis + 1:]
    return array.at[tuple(spot)].set(least).at[tuple(next_to)].set(high)


def steps_of(key, extent, cuts, low, high):
    loudness, own = 1.0, jax.random.fold_in(key, 6)
    for dim, parts in cuts:
        heights = jnp.exp(jax.random.uniform(jax.random.fold_in(own, dim), (parts,), jnp.float32, low / len(cuts), high / len(cuts)))
        loudness = loudness * jnp.repeat(heights, extent[dim] // parts).reshape([-1 if axis == dim else 1 for axis in range(len(extent))])
    return loudness


def noise(stream_key, dims, scale, limit, cuts=(), held_as=jnp.bfloat16):
    drawn = scale * jax.random.normal(stream_key, dims, jnp.float32)
    if cuts:
        drawn = drawn * steps_of(stream_key, dims, cuts, -0.22, 0.18)
    return jnp.clip(drawn, -limit, limit).astype(held_as)


def setup_inputs(seed: int = 0) -> dict:
    seeds = jax.random.split(jax.random.key(seed), 7)
    initial = noise(seeds[0], (REALIZATIONS, NLAT, LON), 1.0, 6.0, ((0, 8), (1, 4)), jnp.float32)
    stencil_numbers = draw_stencil_numbers(jax.random.fold_in(seeds[6], 71), 0)
    innovations = noise(seeds[2], (REALIZATIONS, NOBS), 1.0, 6.0, ((1, 32),), jnp.float32)
    obs_prec = jnp.clip(jnp.exp(math.log(0.5) - 2.3025851 * jax.random.uniform(seeds[3], (NOBS,), jnp.float32) ** steps_of(seeds[3], (NOBS,), ((0, 32),), -0.2, 0.2)), 0.05, 0.5)
    obs_cell = touch_ends(jax.random.randint(seeds[4], (TILE_TOTAL, OB), 0, 128), jax.random.fold_in(seeds[4], 1), 0, 127).astype(jnp.int32)
    band_idx = draw_band_idx(jax.random.fold_in(seeds[6], 71), 0)
    return {"initial": initial, "stencil_numbers": stencil_numbers, "innovations": innovations, "obs_prec": obs_prec, "obs_cell": obs_cell, "band_idx": band_idx}


exact = lax.Precision.HIGHEST


def advance(padded, stencil_numbers):
    centre = padded[:, 1:-1, :]
    north_cell = padded[:, 2:, :]
    south_cell = padded[:, :-2, :]
    east_cell = jnp.roll(centre, -1, axis=2)
    west_cell = jnp.roll(centre, 1, axis=2)
    spread = east_cell + west_cell + north_cell + south_cell - 4.0 * centre
    return centre + stencil_numbers[0] * spread - 0.5 * stencil_numbers[1] * (east_cell - west_cell) - 0.5 * stencil_numbers[2] * (north_cell - south_cell)


def batched_propagation(realization_batch, stencil_numbers):
    fields = realization_batch
    for step_no in range(STEPS):
        fields = advance(jnp.pad(fields, ((0, 0), (1, 1), (0, 0))), stencil_numbers)
    return fields


def reference(initial, stencil_numbers, innovations, obs_prec, obs_cell, band_idx):
    realization_pieces = initial.reshape(N_MEMBER, MEM_DEV, NLAT, LON)
    propagation_operator = lax.map(lambda realization_batch: batched_propagation(realization_batch, stencil_numbers), realization_pieces)
    partition_shape = propagation_operator.reshape(REALIZATIONS, TILE_TOTAL, 128)
    ensemble_mean = jnp.mean(partition_shape, axis=0)
    anomaly = partition_shape - ensemble_mean
    observed = jnp.take_along_axis(anomaly, obs_cell[None, :, :], axis=2)
    weighted = innovations.reshape(REALIZATIONS, TILE_TOTAL, OB) * obs_prec.reshape(TILE_TOTAL, OB)

    def one_block(block_no):
        band_rows = band_idx[block_no]
        distance = jnp.abs(band_rows - block_no).astype(jnp.float32)
        tapers = 1.0 - distance / (R + 1.0)
        obs_band = (observed[:, band_rows, :] * tapers[None, :, None]).reshape(REALIZATIONS, BAND * OB)
        inn_band = weighted[:, band_rows, :].reshape(REALIZATIONS, BAND * OB)
        cells = lax.dynamic_index_in_dim(anomaly, block_no, axis=1, keepdims=False)
        cross_cov = jnp.dot(obs_band.T, cells, precision=exact, preferred_element_type=jnp.float32)
        return jnp.dot(inn_band, cross_cov, precision=exact, preferred_element_type=jnp.float32) / (REALIZATIONS - 1)

    increment = lax.map(one_block, jnp.arange(TILE_TOTAL, dtype=jnp.int32))
    increment = jnp.transpose(increment, (1, 0, 2))
    return (partition_shape + increment).reshape(REALIZATIONS, NLAT, LON)
```

```python
import functools

import jax
import jax.numpy as jnp
from jax import lax
from jax.experimental import pallas as pl
from jax.experimental.pallas import tpu as pltpu
from jax.sharding import PartitionSpec as P

STEPS = 4
OB = 32
R = 8
LANES = 128
VMEM = pl.BlockSpec(memory_space=pltpu.VMEM)
SMEM = pl.BlockSpec(memory_space=pltpu.SMEM)
f32 = jnp.float32
bf16 = jnp.bfloat16


def params(mib):
    return pltpu.CompilerParams(vmem_limit_bytes=mib << 20)


def cost(flops, nbytes):
    return pl.CostEstimate(flops=int(flops), bytes_accessed=int(nbytes), transcendentals=0)


def ceil_div(a, b):
    return -(-a // b)


def partners(count, r):
    if count & (count - 1) == 0:
        return [(i, i ^ r) for i in range(count)]
    return [(i, (i + r) % count) for i in range(count)]


def partner_tables(count, me):
    r = jnp.arange(count, dtype=jnp.int32)
    if count & (count - 1) == 0:
        return me ^ r, me ^ r
    return (me + r) % count, (me - r) % count


def exchange(pieces, axis):
    count = lax.axis_size(axis)
    order = sorted(range(1, count), key=lambda r: -r)
    got = {r: lax.ppermute(pieces[r], axis, partners(count, r)) for r in order}
    return [pieces[0]] + [got[r] for r in range(1, count)]


def exchange_back(pieces, axis):
    count = lax.axis_size(axis)
    order = sorted(range(1, count), key=lambda r: -r)
    got = {
        r: lax.ppermute(pieces[r], axis, [(d, s) for s, d in partners(count, r)]) for r in order
    }
    return [pieces[0]] + [got[r] for r in range(1, count)]


def shift_blocks(block, axis, distance):
    devices = range(lax.axis_size(axis))
    route = [(i - distance, i) for i in devices if i - distance in devices]
    return lax.ppermute(block, axis, route)


def coefficients(numbers):
    k, u, v = numbers
    return (1.0 - 4.0 * k, k - 0.5 * u, k + 0.5 * u, k - 0.5 * v, k + 0.5 * v)


def step_rows(src, dst, coef, first, last, offset):
    def one_row(r, _):
        members, lon = src.shape[1:]
        here = src[r]
        east = pltpu.roll(here, lon - 1, 1)
        west = pltpu.roll(here, 1, 1)
        row = [
            jnp.broadcast_to(coef[i, pl.ds(r + offset, 1), :], (members, lon)) for i in range(5)
        ]
        dst[r] = (
            row[0] * here
            + row[1] * east
            + row[2] * west
            + row[3] * src[r + 1]
            + row[4] * src[r - 1]
        )
        return 0

    lax.fori_loop(first, last, one_row, 0, unroll=2)


def interior_kernel(plan, count, dest, q, numbers, *rest):
    early, rest_out = rest[:count], rest[count]
    buf_a, buf_b, coef = rest[count + 1 :]
    members, rows, _ = q.shape
    tile = rows // count
    for i, c in enumerate(coefficients([numbers[i] for i in range(3)])):
        coef[i] = c

    def turn(g, _):
        r = pl.multiple_of(g * 8, 8)
        buf_a[pl.ds(r, 8)] = jnp.swapaxes(q[:, pl.ds(r, 8), :], 0, 1)
        return 0

    lax.fori_loop(0, rows // 8, turn, 0)
    src, dst = buf_a, buf_b
    for s in range(STEPS):
        step_rows(src, dst, coef, s + 1, rows - s - 1, 0)
        src, dst = dst, src
    for r in range(count):
        base = dest[r] * tile
        for slot, row in enumerate(plan.early):
            early[r][slot] = src[base + row]

    def keep(t, _):
        for slot, row in enumerate(plan.late):
            rest_out[t, slot] = src[t * tile + row]
        return 0

    lax.fori_loop(0, count, keep, 0)


def border_kernel(plan, count, dest, low, high, q_low, q_high, coef_low, coef_high, kept, *rest):
    late = rest[:count]
    buf_a, buf_b, coef, final = rest[count:]
    members = q_low.shape[0]
    wide = 3 * STEPS
    final[...] = kept[...]
    for side, (halo, own, own_coef) in enumerate(
        ((low, q_low, coef_low), (high, q_high, coef_high))
    ):
        strips = (
            [(halo, 0, STEPS), (own, 0, 2 * STEPS)]
            if side == 0
            else [(own, 0, 2 * STEPS), (halo, 0, STEPS)]
        )
        at = 0
        for ref, first, n in strips:
            for r in range(n):
                buf_a[at + r] = ref[:members, first + r, :]
            at += n
        halo_numbers = [halo[members + i] for i in range(3)]
        own_numbers = [own_coef[i] for i in range(3)]
        for i, (h, o) in enumerate(zip(coefficients(halo_numbers), coefficients(own_numbers))):
            parts = [h, o] if side == 0 else [o, h]
            at = 0
            for part in parts:
                coef[i, at : at + part.shape[0], :] = part
                at += part.shape[0]
        src, dst = buf_a, buf_b
        for s in range(STEPS):
            step_rows(src, dst, coef, s + 1, wide - s - 1, 0)
            src, dst = dst, src
        for r in range(STEPS):
            tile, row = plan.where(r if side == 0 else plan.rows - STEPS + r)
            final[tile, plan.late.index(row)] = src[STEPS + r]
    for r in range(count):
        late[r][...] = final[dest[r]]


def split(x):
    high = x.astype(bf16)
    return high, (x - high.astype(f32)).astype(bf16)


def mm(a, b, dims=((1,), (0,))):
    return lax.dot_general(a, b, (dims, ((), ())), preferred_element_type=f32)


def analysis_kernel(plan, count, fresh, old_mix, old_fields, out_rows, keep_fields, *refs):
    refs = list(refs)
    take = lambda n: [refs.pop(0) for _ in range(n)]
    source, rows_of, out_of = take(3)
    pieces = take(count) if fresh else []
    inn, prec, cells = take(3) if fresh else (None, None, None)
    weights = take(1)[0] if out_rows else None
    old_mix_refs = take(len(old_mix))
    old_field_refs = take(len(old_fields))
    mix_out = take(1)[0] if fresh else None
    kept_out = take(1)[0] if keep_fields else None
    outs = take(count) if out_rows else []
    mix, fields = take(2)
    tile = plan.tile
    members, lon = fields.shape[1:]
    share = members // count
    group = LANES // OB
    pack = plan.pack
    per_row = lon // LANES
    pairs = per_row // pack
    for slots, ref in zip(old_mix, old_mix_refs):
        for row, slot in slots:
            mix[row + 1] = ref[slot]
    for slots, ref in zip(old_fields, old_field_refs):
        for row, slot in slots:
            fields[row] = ref[slot]
    if fresh:
        for r in range(count):
            first = pl.multiple_of(source[r] * share, share)
            for slot, row in enumerate(fresh):
                fields[row, pl.ds(first, share), :] = pieces[r][slot]

        def observe(slot, _):
            row = rows_of[slot]
            for q in range(per_row // group):
                anomalies = []
                for t in range(group):
                    lanes = slice((q * group + t) * LANES, (q * group + t + 1) * LANES)
                    block = fields[row, :, lanes]
                    anomalies.append(block - jnp.mean(block, axis=0, keepdims=True))
                high, low = split(jnp.concatenate(anomalies, axis=0))
                at = row * (per_row // group) + q
                cell_row = cells[pl.ds(at, 1), :]
                chosen = (
                    lax.broadcasted_iota(jnp.int32, (LANES, LANES), 0)
                    == jnp.broadcast_to(cell_row, (LANES, LANES))
                )
                pick = jnp.where(chosen, 1.0, 0.0).astype(bf16)
                seen = mm(high, pick) + mm(low, pick)
                shape = seen.shape
                same = (
                    lax.broadcasted_iota(jnp.int32, shape, 0) // members
                    == lax.broadcasted_iota(jnp.int32, shape, 1) // OB
                )
                seen_high, seen_low = split(jnp.where(same, seen, 0.0))
                lanes = pl.ds(pl.multiple_of(at * LANES, LANES), LANES)
                weighted = inn[:, lanes] * prec[:, lanes]
                w_high, w_low = split(weighted)
                both = mm(
                    jnp.concatenate([w_high, w_low], axis=0), seen_high, ((1,), (1,))
                )
                total = both[:members] + both[members:] + mm(w_high, seen_low, ((1,), (1,)))
                wide = pack * members
                for k in range(group // pack):
                    mix[row + 1, q * (group // pack) + k] = total[:, k * wide : (k + 1) * wide]
            return 0

        lax.fori_loop(0, len(fresh), observe, 0)
        for slot, row in enumerate(fresh):
            mix_out[slot] = mix[row + 1]
    for slot, row in enumerate(keep_fields):
        kept_out[slot] = fields[row]
    if out_rows:
        reach = ceil_div(R, pack)
        width = 2 * reach + 1

        def update(slot, _):
            row = out_of[slot]
            for pair in range(pairs):
                sums = [jnp.zeros((members, pack * members), f32) for _ in range(pack)]
                for d in range(width):
                    place = pair + d - reach
                    step = place // pairs
                    part = mix[row + 1 + step, place - step * pairs]
                    for t in range(pack):
                        block = row * per_row + pair * pack + t
                        w = weights[block, pl.ds(d, 1), :]
                        sums[t] += part * jnp.broadcast_to(w, part.shape)
                for t in range(pack):
                    first = (pair * pack + t) * LANES
                    cells_here = fields[row, :, first : first + LANES]
                    anomaly = cells_here - jnp.mean(cells_here, axis=0, keepdims=True)
                    a_high, a_low = split(anomaly)
                    a_high = jnp.concatenate([a_high] * pack, axis=0)
                    a_low = jnp.concatenate([a_low] * pack, axis=0)
                    s_high, s_low = split(sums[t])
                    both = mm(jnp.concatenate([s_high, s_low], axis=0), a_high)
                    done = cells_here + both[:members] + both[members:] + mm(s_high, a_low)
                    fields[row, :, first : first + LANES] = done
            return 0

        lax.fori_loop(0, len(out_rows), update, 0)
        for r in range(count):
            first = pl.multiple_of(source[r] * share, share)
            for slot, row in enumerate(out_rows):
                outs[r][slot] = fields[row, pl.ds(first, share), :]


def assemble_kernel(plan, count, parts, source, *refs):
    pieces, (out, buf) = refs[:-2], refs[-2:]
    at = 0
    for rows in parts:
        for r in range(count):
            base = source[r] * plan.tile
            for slot, row in enumerate(rows):
                buf[base + row] = pieces[at + r][slot]
        at += count

    def turn(g, _):
        r = pl.multiple_of(g * 8, 8)
        out[:, pl.ds(r, 8), :] = jnp.swapaxes(buf[pl.ds(r, 8)], 0, 1)
        return 0

    lax.fori_loop(0, plan.rows // 8, turn, 0)


class Plan:
    def __init__(self, rows, count, members):
        self.rows = rows
        self.count = count
        self.tile = rows // count
        self.members = members
        self.pack = max(1, LANES // members)
        tile = self.tile
        self.early = [r for r in range(tile) if STEPS <= r < tile - STEPS]
        self.late = [r for r in range(tile) if r not in self.early]

    def where(self, row):
        return row // self.tile, row % self.tile


def shards(initial, stencil_numbers, innovations, obs_prec, obs_cell, band_idx):
    share, rows, lon = initial.shape
    count = lax.axis_size("member")
    members = share * count
    plan = Plan(rows, count, members)
    tile, pack = plan.tile, plan.pack
    per_row = lon // LANES
    pairs = per_row // pack
    me = lax.axis_index("member")
    dest, source = partner_tables(count, me)
    sds = lambda *shape: jax.ShapeDtypeStruct(shape, f32)
    ints = lambda values: jnp.array(list(values) or [0], jnp.int32)

    stacked_low = jnp.concatenate([initial[:, :STEPS], stencil_numbers[:, :STEPS]], axis=0)
    stacked_high = jnp.concatenate([initial[:, -STEPS:], stencil_numbers[:, -STEPS:]], axis=0)
    low = shift_blocks(stacked_high, "slab", 1)
    high = shift_blocks(stacked_low, "slab", -1)

    early_rows, late_rows = len(plan.early), len(plan.late)
    outs = pl.pallas_call(
        functools.partial(interior_kernel, plan, count),
        out_shape=[sds(max(early_rows, 1), share, lon)] * count
        + [sds(count, late_rows, share, lon)],
        in_specs=[SMEM, VMEM, VMEM],
        out_specs=[VMEM] * (count + 1),
        scratch_shapes=[
            pltpu.VMEM((rows, share, lon), f32),
            pltpu.VMEM((rows, share, lon), f32),
            pltpu.VMEM((5, rows, lon), f32),
        ],
        compiler_params=params(40),
        cost_estimate=cost(11 * STEPS * initial.size, 8 * initial.size),
        name="interior",
    )(dest, initial, stencil_numbers)
    early, kept = outs[:count], outs[count]
    if plan.early:
        early = exchange(early, "member")

    late = pl.pallas_call(
        functools.partial(border_kernel, plan, count),
        out_shape=[sds(late_rows, share, lon)] * count,
        in_specs=[SMEM] + [VMEM] * 7,
        out_specs=[VMEM] * count,
        scratch_shapes=[
            pltpu.VMEM((3 * STEPS, share, lon), f32),
            pltpu.VMEM((3 * STEPS, share, lon), f32),
            pltpu.VMEM((5, 3 * STEPS, lon), f32),
            pltpu.VMEM((count, late_rows, share, lon), f32),
        ],
        compiler_params=params(40),
        cost_estimate=cost(11 * STEPS * initial.size // 4, 4 * initial.size),
        name="border",
    )(
        dest,
        low,
        high,
        initial[:, : 2 * STEPS],
        initial[:, -2 * STEPS :],
        stencil_numbers[:, : 2 * STEPS],
        stencil_numbers[:, -2 * STEPS :],
        kept,
    )
    late = exchange(late, "member")

    blocks = tile * per_row
    first_block = lax.axis_index(("slab", "member")) * blocks
    own = first_block + jnp.arange(blocks, dtype=jnp.int32)
    reach = ceil_div(R, pack)
    width = 2 * reach + 1
    start = own // pack * pack - reach * pack
    reached = start[:, None] + jnp.arange(width * pack, dtype=jnp.int32)
    in_band = jnp.any(reached[:, :, None] == band_idx[:, None, :], axis=2)
    distance = jnp.abs(reached - own[:, None]).astype(f32)
    tapers = jnp.where(in_band, 1.0 - distance / (R + 1.0), 0.0) / (members - 1)
    weights = jnp.repeat(tapers, members, axis=1).reshape(blocks, width, pack * members)
    prec = obs_prec.reshape(1, -1)
    cells = obs_cell.reshape(-1, LANES)

    def analyse(fresh, pieces, old_mix, old_fields, out_rows, keep_fields, name):
        args = [source, ints(fresh), ints(out_rows)]
        specs = [SMEM] * 3
        shapes = []
        if fresh:
            args += [*pieces, innovations, prec, cells]
            shapes += [sds(len(fresh), pairs, members, pack * members)]
        if out_rows:
            args += [weights]
        args += [m[1] for m in old_mix] + [f[1] for f in old_fields]
        if keep_fields:
            shapes += [sds(len(keep_fields), members, lon)]
        if out_rows:
            shapes += [sds(len(out_rows), share, lon)] * count
        specs += [VMEM] * (len(args) - 3)
        got = list(
            pl.pallas_call(
                functools.partial(
                    analysis_kernel,
                    plan,
                    count,
                    fresh,
                    [m[0] for m in old_mix],
                    [f[0] for f in old_fields],
                    out_rows,
                    keep_fields,
                ),
                out_shape=shapes,
                in_specs=specs,
                out_specs=[VMEM] * len(shapes),
                scratch_shapes=[
                    pltpu.VMEM((tile + 2, pairs, members, pack * members), f32),
                    pltpu.VMEM((tile, members, lon), f32),
                ],
                compiler_params=params(56),
                cost_estimate=cost(
                    (len(fresh) + len(out_rows)) * 6 * members * members * lon,
                    4 * members * lon * (len(fresh) + 2 * len(out_rows)),
                ),
                name=name,
            )(*args)
        )
        mixing = got.pop(0) if fresh else None
        kept_fields = got.pop(0) if keep_fields else None
        return mixing, kept_fields, got

    slots = lambda rows: [(row, slot) for slot, row in enumerate(rows)]
    parts, returned = [], []
    rims = sorted({0, tile - 1})
    inner = [r for r in plan.early if r - 1 in plan.early and r + 1 in plan.early]
    old_mix, old_fields = [], []
    if plan.early:
        edge = [r for r in plan.early if r not in inner]
        mixing, fields, back = analyse(plan.early, early, [], [], inner, edge, "analyse_early")
        old_mix = [(slots(plan.early), mixing)]
        old_fields = [(slots(edge), fields)] if edge else []
        if inner:
            parts.append(inner)
            returned += exchange_back(back, "member")
    middle = [r for r in range(tile) if r not in inner and r not in rims]
    mixing, fields, back = analyse(
        plan.late, late, old_mix, old_fields, middle, rims, "analyse_late"
    )
    axes = ("slab", "member")
    from_prev = shift_blocks(mixing[plan.late.index(tile - 1)][None], axes, 1)
    from_next = shift_blocks(mixing[plan.late.index(0)][None], axes, -1)
    if middle:
        parts.append(middle)
        returned += exchange_back(back, "member")
    near = sorted({row for r in rims for row in (r - 1, r, r + 1) if 0 <= row < tile})
    near_late = [r for r in near if r in plan.late]
    held = [([(-1, 0)], from_prev), ([(tile, 0)], from_next)]
    held.append(([(row, plan.late.index(row)) for row in near_late], mixing))
    _, _, back = analyse([], [], held, [(slots(rims), fields)], rims, [], "analyse_rims")
    parts.append(rims)
    returned += exchange_back(back, "member")

    return pl.pallas_call(
        functools.partial(assemble_kernel, plan, count, parts),
        out_shape=sds(share, rows, lon),
        in_specs=[SMEM] + [VMEM] * len(returned),
        out_specs=VMEM,
        scratch_shapes=[pltpu.VMEM((rows, share, lon), f32)],
        compiler_params=params(40),
        cost_estimate=cost(0, 8 * initial.size),
        name="assemble",
    )(source, *returned)


def solution(mesh):
    in_specs = (
        P("member", "slab", None),
        P(None, "slab", None),
        P(None, ("slab", "member")),
        P(("slab", "member")),
        P(("slab", "member"), None),
        P(("slab", "member"), None),
    )
    out_specs = P("member", "slab", None)
    return jax.shard_map(shards, mesh=mesh, in_specs=in_specs, out_specs=out_specs, check_vma=False)
```

```python
import functools

import jax
import jax.numpy as jnp
from jax import lax
from jax.experimental import pallas as pl
from jax.experimental.pallas import tpu as pltpu
from jax.sharding import PartitionSpec as P

STEPS = 4
OB = 32
R = 8
LANES = 128
BATCH = 16
SECTIONS = 2
FLIGHT = 5
SECTION_MIB = 58
BORDER_MIB = 32
ANALYSIS_MIB = 56
VMEM = pl.BlockSpec(memory_space=pltpu.VMEM)
SMEM = pl.BlockSpec(memory_space=pltpu.SMEM)
HBM = pl.BlockSpec(memory_space=pltpu.HBM)
f32 = jnp.float32
bf16 = jnp.bfloat16
SHORT = ("mix_rims", "mix_late", "analyse_late")


def hint(us=0):
    return pl.CostEstimate(flops=0, bytes_accessed=int(us * 3.69e6), transcendentals=0)


def params(mib):
    return pltpu.CompilerParams(vmem_limit_bytes=mib << 20)


def ceil_div(a, b):
    return -(-a // b)


def after(value, *earlier):
    return lax.optimization_barrier((value, *earlier))[0]


class Chain:
    def __init__(self, flight):
        self.flight = flight
        self.ended = []

    def permute(self, piece, axis, route):
        if len(self.ended) >= self.flight:
            piece = after(piece, self.ended[-self.flight])
        self.ended.append(lax.ppermute(piece, axis, route))
        return self.ended[-1]

    def swap(self, piece, r):
        return self.permute(piece, "member", [(i, i ^ r) for i in range(lax.axis_size("member"))])

    def shift(self, block, axis, distance):
        devices = range(lax.axis_size(axis))
        route = [(i - distance, i) for i in devices if i - distance in devices]
        return self.permute(block, axis, route)


def coefficients(numbers):
    k, u, v = numbers
    return (1.0 - 4.0 * k, k - 0.5 * u, k + 0.5 * u, k - 0.5 * v, k + 0.5 * v)


def step_rows(src, dst, coef, first, last, offset):
    members, lon = src.shape[1:]

    def one_row(r):
        here = src[r]
        east = pltpu.roll(here, lon - 1, 1)
        west = pltpu.roll(here, 1, 1)
        row = [
            jnp.broadcast_to(coef[i, pl.ds(r + offset, 1), :], (members, lon)) for i in range(5)
        ]
        dst[r] = (
            row[0] * here
            + row[1] * east
            + row[2] * west
            + row[3] * src[r + 1]
            + row[4] * src[r - 1]
        )

    def some_rows(g, _):
        for i in range(BATCH):
            one_row(first + g * BATCH + i)
        return 0

    batches = (last - first) // BATCH
    lax.fori_loop(0, batches, some_rows, 0)
    for r in range(first + batches * BATCH, last):
        one_row(r)


def section_kernel(plan, section, place, q, numbers, *refs):
    refs = list(refs)
    size = plan.size
    early = [refs.pop(0) for _ in range(size)] if plan.early else []
    kept = refs.pop(0)
    halos = [refs.pop(0) for _ in range(2)] if section else []
    edges = [refs.pop(0) for _ in range(4)] if section else []
    q_win, n_win, buf_a, buf_b, coef, sems = refs
    members, window, lon = q_win.shape
    height = size * plan.tile
    base = place[section] * height
    start = pl.multiple_of(jnp.clip(base - 8, 0, plan.rows - window), 8)
    copies = [
        pltpu.make_async_copy(numbers.at[:, pl.ds(start, window), :], n_win, sems.at[0]),
        pltpu.make_async_copy(q.at[:, pl.ds(start, window), :], q_win, sems.at[1]),
    ]
    for i, first in enumerate((0, plan.rows - 8)) if section else []:
        rows = pl.ds(first, 8)
        copies.append(pltpu.make_async_copy(q.at[:, rows, :], edges[2 * i], sems.at[2 + 2 * i]))
        copies.append(
            pltpu.make_async_copy(numbers.at[:, rows, :], edges[2 * i + 1], sems.at[3 + 2 * i])
        )
    for copy in copies:
        copy.start()
    copies[0].wait()
    for i, c in enumerate(coefficients([n_win[i] for i in range(3)])):
        coef[i, 8 : 8 + window, :] = c
    copies[1].wait()
    shift = base - 8 - start

    def turn(g):
        at = pl.multiple_of(jnp.clip(g * 8 + shift, 0, window - 8), 8)
        return jnp.swapaxes(q_win[:, pl.ds(at, 8), :], 0, 1)

    def some_turns(g, _):
        buf_a[pl.ds(g * 8 - 4, 8)] = turn(g)
        return 0

    groups = height // 8 + 2
    buf_a[0:4] = turn(0)[4:]
    lax.fori_loop(1, groups - 1, some_turns, 0)
    buf_a[height + 4 : height + 8] = turn(groups - 1)[:4]
    src, dst = buf_a, buf_b
    for s in range(STEPS):
        step_rows(src, dst, coef, s + 1, height + 7 - s, shift + 12)
        src, dst = dst, src
    for i in range(size):
        r = section * size + i
        first = STEPS + (place[section] * size ^ r ^ place[plan.sections]) % size * plan.tile
        for slot, row in enumerate(plan.early):
            early[i][slot] = src[first + row]
        for slot, row in enumerate(plan.late):
            kept[i, slot] = src[first + row]
    for copy in copies[2:]:
        copy.wait()
    for side in range(2) if section else []:
        first = 0 if side == 0 else 8 - STEPS
        fields, stencil = edges[2 * side : 2 * side + 2]
        turned = jnp.swapaxes(fields[...], 0, 1)
        for row in range(STEPS):
            halos[side][row, :members] = turned[first + row]
            halos[side][row, members:] = jnp.zeros_like(halos[side][row, members:])
            for i in range(3):
                halos[side][row, members + i : members + i + 1] = stencil[
                    i, first + row : first + row + 1
                ]


def border_kernel(plan, place, low, high, q, numbers, *refs):
    kept = refs[: plan.sections]
    late = refs[plan.sections : plan.sections + plan.count]
    q_edge, n_edge, buf_a, buf_b, coef, final, sems = refs[plan.sections + plan.count :]
    me = place[plan.sections]
    members = q_edge.shape[1]
    wide = 3 * STEPS
    copies = []
    for side, first in enumerate((0, plan.rows - 2 * STEPS)):
        rows = pl.ds(first, 2 * STEPS)
        copies += [
            pltpu.make_async_copy(q.at[:, rows, :], q_edge.at[side], sems.at[2 * side]),
            pltpu.make_async_copy(numbers.at[:, rows, :], n_edge.at[side], sems.at[2 * side + 1]),
        ]
    for copy in copies:
        copy.start()
    for section in range(plan.sections):
        final[section * plan.size : (section + 1) * plan.size] = kept[section][...]
    for copy in copies:
        copy.wait()
    for side, halo in enumerate((low, high)):
        halo_at, own_at = (0, STEPS) if side == 0 else (2 * STEPS, 0)
        buf_a[halo_at : halo_at + STEPS] = halo[:, :members, :]
        buf_a[own_at : own_at + 2 * STEPS] = jnp.swapaxes(q_edge[side], 0, 1)
        halo_numbers = [halo[:, members + i, :] for i in range(3)]
        own_numbers = [n_edge[side, i] for i in range(3)]
        for i, (h, o) in enumerate(zip(coefficients(halo_numbers), coefficients(own_numbers))):
            coef[i, halo_at : halo_at + STEPS, :] = h
            coef[i, own_at : own_at + 2 * STEPS, :] = o
        src, dst = buf_a, buf_b
        for s in range(STEPS):
            step_rows(src, dst, coef, s + 1, wide - s - 1, 0)
            src, dst = dst, src
        for r in range(STEPS):
            row = r if side == 0 else plan.rows - STEPS + r
            final[me ^ (row // plan.tile), plan.late.index(row % plan.tile)] = src[STEPS + r]
    for r in range(plan.count):
        late[r][...] = final[r]


def split(x):
    high = x.astype(bf16)
    return high, (x - high.astype(f32)).astype(bf16)


def mm(a, b, dims=((1,), (0,))):
    return lax.dot_general(a, b, (dims, ((), ())), preferred_element_type=f32)


def analysis_kernel(plan, arrived, fresh, old_mix, old_fields, out_rows, keep_fields, *refs):
    refs = list(refs)
    count = plan.count
    take = lambda n: [refs.pop(0) for _ in range(n)]
    place, fresh_of, out_of = take(3)
    me = place[plan.sections]
    pieces = take(count) if arrived else []
    inn, prec, cells = take(3) if fresh else (None, None, None)
    weights = take(1)[0] if out_rows else None
    old_mix_refs = take(len(old_mix))
    old_field_refs = take(len(old_fields))
    mix_out = take(1)[0] if fresh else None
    kept_out = take(1)[0] if keep_fields else None
    outs = take(count) if out_rows else []
    mix, fields = take(2)
    tile = plan.tile
    members, lon = fields.shape[1:]
    share = members // count
    group = LANES // OB
    pack = plan.pack
    per_row = lon // LANES
    pairs = per_row // pack
    for slots, ref in zip(old_mix, old_mix_refs):
        for row, slot in slots:
            mix[row + 1] = ref[slot]
    for slots, ref in zip(old_fields, old_field_refs):
        for row, slot in slots:
            fields[row] = ref[slot]
    if arrived:
        for r in range(count):
            first = pl.multiple_of((me ^ r) * share, share)
            for slot, row in enumerate(arrived):
                fields[row, pl.ds(first, share), :] = pieces[r][slot]
    if fresh:

        def observe(slot, _):
            row = fresh_of[slot]
            for q in range(per_row // group):
                anomalies = []
                for t in range(group):
                    lanes = slice((q * group + t) * LANES, (q * group + t + 1) * LANES)
                    block = fields[row, :, lanes]
                    anomalies.append(block - jnp.mean(block, axis=0, keepdims=True))
                high, low = split(jnp.concatenate(anomalies, axis=0))
                at = row * (per_row // group) + q
                cell_row = cells[pl.ds(at, 1), :]
                chosen = (
                    lax.broadcasted_iota(jnp.int32, (LANES, LANES), 0)
                    == jnp.broadcast_to(cell_row, (LANES, LANES))
                )
                pick = jnp.where(chosen, 1.0, 0.0).astype(bf16)
                seen = mm(high, pick) + mm(low, pick)
                shape = seen.shape
                same = (
                    lax.broadcasted_iota(jnp.int32, shape, 0) // members
                    == lax.broadcasted_iota(jnp.int32, shape, 1) // OB
                )
                seen_high, seen_low = split(jnp.where(same, seen, 0.0))
                lanes = pl.ds(pl.multiple_of(at * LANES, LANES), LANES)
                weighted = inn[:, lanes] * prec[:, lanes]
                w_high, w_low = split(weighted)
                both = mm(
                    jnp.concatenate([w_high, w_low], axis=0), seen_high, ((1,), (1,))
                )
                total = both[:members] + both[members:] + mm(w_high, seen_low, ((1,), (1,)))
                wide = pack * members
                for k in range(group // pack):
                    mix[row + 1, q * (group // pack) + k] = total[:, k * wide : (k + 1) * wide]
            return 0

        lax.fori_loop(0, len(fresh), observe, 0)
        for slot, row in enumerate(fresh):
            mix_out[slot] = mix[row + 1]
    for slot, row in enumerate(keep_fields):
        kept_out[slot] = fields[row]
    if out_rows:
        reach = ceil_div(R, pack)
        width = 2 * reach + 1

        def update(slot, _):
            row = out_of[slot]
            for pair in range(pairs):
                sums = [jnp.zeros((members, pack * members), f32) for _ in range(pack)]
                for d in range(width):
                    place = pair + d - reach
                    step = place // pairs
                    part = mix[row + 1 + step, place - step * pairs]
                    for t in range(pack):
                        block = row * per_row + pair * pack + t
                        w = weights[block, pl.ds(d, 1), :]
                        sums[t] += part * jnp.broadcast_to(w, part.shape)
                for t in range(pack):
                    first = (pair * pack + t) * LANES
                    cells_here = fields[row, :, first : first + LANES]
                    anomaly = cells_here - jnp.mean(cells_here, axis=0, keepdims=True)
                    a_high, a_low = split(anomaly)
                    a_high = jnp.concatenate([a_high] * pack, axis=0)
                    a_low = jnp.concatenate([a_low] * pack, axis=0)
                    s_high, s_low = split(sums[t])
                    both = mm(jnp.concatenate([s_high, s_low], axis=0), a_high)
                    done = cells_here + both[:members] + both[members:] + mm(s_high, a_low)
                    fields[row, :, first : first + LANES] = done
            return 0

        lax.fori_loop(0, len(out_rows), update, 0)
        for r in range(count):
            first = pl.multiple_of((me ^ r) * share, share)
            for slot, row in enumerate(out_rows):
                outs[r][slot] = fields[row, pl.ds(first, share), :]


def assemble_kernel(plan, parts, place, *refs):
    pieces, (out, buf) = refs[:-2], refs[-2:]
    me = place[plan.sections]
    at = 0
    for rows in parts:
        for r in range(plan.count):
            base = (me ^ r) * plan.tile
            for slot, row in enumerate(rows):
                buf[base + row] = pieces[at + r][slot]
        at += plan.count

    def turn(g, _):
        r = pl.multiple_of(g * 8, 8)
        out[:, pl.ds(r, 8), :] = jnp.swapaxes(buf[pl.ds(r, 8)], 0, 1)
        return 0

    lax.fori_loop(0, plan.rows // 8, turn, 0)


class Plan:
    def __init__(self, rows, count, members, sections):
        assert count >= 4 and count & (count - 1) == 0
        self.rows = rows
        self.count = count
        self.sections = sections
        self.size = count // self.sections
        self.tile = rows // count
        self.pack = max(1, LANES // members)
        self.early = [r for r in range(self.tile) if STEPS <= r < self.tile - STEPS]
        self.late = [r for r in range(self.tile) if r not in self.early]


def shards(initial, stencil_numbers, innovations, obs_prec, obs_cell, band_idx):
    share, rows, lon = initial.shape
    count = lax.axis_size("member")
    members = share * count
    plan = Plan(rows, count, members, SECTIONS)
    tile, pack, size = plan.tile, plan.pack, plan.size
    per_row = lon // LANES
    pairs = per_row // pack
    me = lax.axis_index("member")
    place = jnp.stack([me // size ^ i for i in range(plan.sections)] + [me]).astype(jnp.int32)
    sds = lambda *shape: jax.ShapeDtypeStruct(shape, f32)
    ints = lambda values: jnp.array(list(values) or [0], jnp.int32)

    early_rows, late_rows = len(plan.early), len(plan.late)
    height = size * tile
    window = min(rows, height + (8 if plan.sections == 2 else 16))
    chain = Chain(FLIGHT)
    half = count // 2
    far, near = list(reversed(range(half, count))), list(reversed(range(1, half)))
    turns = far[:2]
    for i in range(half):
        turns += near[i : i + 1] + far[i + 2 : i + 3]

    def send(pieces, partners, *earlier):
        got = list(pieces)
        for r in partners:
            piece = after(pieces[r], *earlier) if earlier and r == partners[-1] else pieces[r]
            got[r] = chain.swap(piece, r)
        return got

    def forecast(section, order):
        shapes = []
        if plan.early:
            shapes = [sds(early_rows, share, lon)] * size
        shapes.append(sds(size, late_rows, share, lon))
        scratch = []
        if section:
            shapes += [sds(STEPS, share + 8, lon)] * 2
            scratch = [pltpu.VMEM((share, 8, lon), f32), pltpu.VMEM((3, 8, lon), f32)] * 2
        return pl.pallas_call(
            functools.partial(section_kernel, plan, section),
            out_shape=shapes,
            in_specs=[SMEM, HBM, HBM],
            out_specs=[VMEM] * len(shapes),
            scratch_shapes=scratch
            + [
                pltpu.VMEM((share, window, lon), f32),
                pltpu.VMEM((3, window, lon), f32),
                pltpu.VMEM((height + 8, share, lon), f32),
                pltpu.VMEM((height + 8, share, lon), f32),
                pltpu.VMEM((5, window + 16, lon), f32),
                pltpu.SemaphoreType.DMA((6,)),
            ],
            compiler_params=params(SECTION_MIB),
            cost_estimate=hint(9),
            name=f"section_{section}",
        )(order, initial, stencil_numbers)

    far_outs = forecast(1, place)
    near_outs = forecast(0, after(place, far_outs[-1]))
    kept_far, kept_near = far_outs[-3], near_outs[-1]
    if plan.early:
        early = near_outs[:size] + far_outs[:size]
        low = chain.shift(far_outs[-1], "slab", 1)
        early = send(early, far[:2])
        high = chain.shift(far_outs[-2], "slab", -1)
        early = send(early, far[2:3] + [r for r in turns[2:] if r != far[2]])
    else:
        low = chain.shift(far_outs[-1], "slab", 1)
        high = chain.shift(far_outs[-2], "slab", -1)
    late = pl.pallas_call(
        functools.partial(border_kernel, plan),
        out_shape=[sds(late_rows, share, lon)] * count,
        in_specs=[SMEM, VMEM, VMEM, HBM, HBM] + [VMEM] * plan.sections,
        out_specs=[VMEM] * count,
        scratch_shapes=[
            pltpu.VMEM((2, share, 2 * STEPS, lon), f32),
            pltpu.VMEM((2, 3, 2 * STEPS, lon), f32),
            pltpu.VMEM((3 * STEPS, share, lon), f32),
            pltpu.VMEM((3 * STEPS, share, lon), f32),
            pltpu.VMEM((5, 3 * STEPS, lon), f32),
            pltpu.VMEM((count, late_rows, share, lon), f32),
            pltpu.SemaphoreType.DMA((4,)),
        ],
        compiler_params=params(BORDER_MIB),
        cost_estimate=hint(4),
        name="border",
    )(place, low, high, initial, stencil_numbers, kept_near, kept_far)

    blocks = tile * per_row
    first_block = lax.axis_index(("slab", "member")) * blocks
    own = first_block + jnp.arange(blocks, dtype=jnp.int32)
    reach = ceil_div(R, pack)
    width = 2 * reach + 1
    start = own // pack * pack - reach * pack
    reached = start[:, None] + jnp.arange(width * pack, dtype=jnp.int32)
    in_band = jnp.any(reached[:, :, None] == band_idx[:, None, :], axis=2)
    distance = jnp.abs(reached - own[:, None]).astype(f32)
    tapers = jnp.where(in_band, 1.0 - distance / (R + 1.0), 0.0) / (members - 1)
    weights = jnp.repeat(tapers, members, axis=1).reshape(blocks, width, pack * members)
    prec = obs_prec.reshape(1, -1)
    cells = obs_cell.reshape(-1, LANES)

    def analyse(arrived, pieces, fresh, old_mix, old_fields, out_rows, keep_fields, name, order=place):
        args = [order, ints(fresh), ints(out_rows)]
        shapes = []
        if arrived:
            args += pieces
        if fresh:
            args += [innovations, prec, cells]
            shapes += [sds(len(fresh), pairs, members, pack * members)]
        if out_rows:
            args += [weights]
        args += [m[1] for m in old_mix] + [f[1] for f in old_fields]
        if keep_fields:
            shapes += [sds(len(keep_fields), members, lon)]
        if out_rows:
            shapes += [sds(len(out_rows), share, lon)] * count
        made = list(
            pl.pallas_call(
                functools.partial(
                    analysis_kernel,
                    plan,
                    arrived,
                    fresh,
                    [m[0] for m in old_mix],
                    [f[0] for f in old_fields],
                    out_rows,
                    keep_fields,
                ),
                out_shape=shapes,
                in_specs=[SMEM] * 3 + [VMEM] * (len(args) - 3),
                out_specs=[VMEM] * len(shapes),
                scratch_shapes=[
                    pltpu.VMEM((tile + 2, pairs, members, pack * members), f32),
                    pltpu.VMEM((tile, members, lon), f32),
                ],
                compiler_params=params(ANALYSIS_MIB),
                cost_estimate=hint(0 if name in SHORT else 1.2 * len(fresh)),
                name=name,
            )(*args)
        )
        mixing = made.pop(0) if fresh else None
        fields = made.pop(0) if keep_fields else None
        return mixing, fields, made

    slots = lambda rows: [(row, slot) for slot, row in enumerate(rows)]
    parts, returned = [], []
    inner = [r for r in plan.early if r - 1 in plan.early and r + 1 in plan.early]
    old_mix, old_fields, order = [], [], place
    if plan.early:
        edge = [r for r in plan.early if r not in inner]
        mixing, fields, back = analyse(
            plan.early, early, plan.early, [], [], inner, edge, "analyse_early"
        )
        old_mix = [(slots(plan.early), mixing)]
        old_fields = [(slots(edge), fields)] if edge else []
        late = send(late, turns, fields if edge else mixing)
        order = after(place, mixing)
        if inner:
            parts.append(inner)
            back = send(back, far[:2])
    else:
        late = send(late, turns)
    rims = sorted({0, tile - 1})
    rest = [r for r in plan.late if r not in rims]
    mixing, _, _ = analyse(plan.late, late, rims, [], [], [], [], "mix_rims", order)
    axes = ("slab", "member")
    from_prev = chain.shift(mixing[rims.index(tile - 1)][None], axes, 1)
    from_next = chain.shift(mixing[0][None], axes, -1)
    if inner:
        returned += send(back, far[2:] + near)
    old_mix += [(slots(rims), mixing), ([(-1, 0)], from_prev), ([(tile, 0)], from_next)]
    if rest:
        mixing, _, _ = analyse(plan.late, late, rest, [], [], [], [], "mix_late", after(place, mixing))
        old_mix += [(slots(rest), mixing)]
    others = [r for r in range(tile) if r not in inner]
    _, _, back = analyse(plan.late, late, [], old_mix, old_fields, others, [], "analyse_late")
    parts.append(others)
    returned += send(back, turns)

    return pl.pallas_call(
        functools.partial(assemble_kernel, plan, parts),
        out_shape=sds(share, rows, lon),
        in_specs=[SMEM] + [VMEM] * len(returned),
        out_specs=VMEM,
        scratch_shapes=[pltpu.VMEM((rows, share, lon), f32)],
        compiler_params=params(32),
        cost_estimate=hint(4),
        name="assemble",
    )(place, *returned)


def solution(mesh):
    in_specs = (
        P("member", "slab", None),
        P(None, "slab", None),
        P(None, ("slab", "member")),
        P(("slab", "member")),
        P(("slab", "member"), None),
        P(("slab", "member"), None),
    )
    out_specs = P("member", "slab", None)
    return jax.shard_map(shards, mesh=mesh, in_specs=in_specs, out_specs=out_specs, check_vma=False)
```

```python
import functools

import jax
import jax.numpy as jnp
from jax import lax
from jax.experimental import pallas as pl
from jax.experimental.pallas import tpu as pltpu
from jax.sharding import PartitionSpec as P

STEPS = 4
OB = 32
R = 8
LANES = 128
BATCH = 16
SECTIONS = 4
FLIGHT = 5
SECTION_MIB = 58
BORDER_MIB = 32
ANALYSIS_MIB = 56
VMEM = pl.BlockSpec(memory_space=pltpu.VMEM)
SMEM = pl.BlockSpec(memory_space=pltpu.SMEM)
HBM = pl.BlockSpec(memory_space=pltpu.HBM)
f32 = jnp.float32
bf16 = jnp.bfloat16
SHORT = ("mix_rims", "mix_late", "analyse_late")


def hint(us=0):
    return pl.CostEstimate(flops=0, bytes_accessed=int(us * 3.69e6), transcendentals=0)


def params(mib):
    return pltpu.CompilerParams(vmem_limit_bytes=mib << 20)


def ceil_div(a, b):
    return -(-a // b)


def after(value, *earlier):
    return lax.optimization_barrier((value, *earlier))[0]


class Chain:
    def __init__(self, flight):
        self.flight = flight
        self.ended = []

    def permute(self, piece, axis, route):
        if len(self.ended) >= self.flight:
            piece = after(piece, self.ended[-self.flight])
        self.ended.append(lax.ppermute(piece, axis, route))
        return self.ended[-1]

    def swap(self, piece, r):
        return self.permute(piece, "member", [(i, i ^ r) for i in range(lax.axis_size("member"))])

    def shift(self, block, axis, distance):
        devices = range(lax.axis_size(axis))
        route = [(i - distance, i) for i in devices if i - distance in devices]
        return self.permute(block, axis, route)


def coefficients(numbers):
    k, u, v = numbers
    return (1.0 - 4.0 * k, k - 0.5 * u, k + 0.5 * u, k - 0.5 * v, k + 0.5 * v)


def step_rows(src, dst, coef, first, last, offset):
    members, lon = src.shape[1:]

    def one_row(r):
        here = src[r]
        east = pltpu.roll(here, lon - 1, 1)
        west = pltpu.roll(here, 1, 1)
        row = [
            jnp.broadcast_to(coef[i, pl.ds(r + offset, 1), :], (members, lon)) for i in range(5)
        ]
        dst[r] = (
            row[0] * here
            + row[1] * east
            + row[2] * west
            + row[3] * src[r + 1]
            + row[4] * src[r - 1]
        )

    def some_rows(g, _):
        for i in range(BATCH):
            one_row(first + g * BATCH + i)
        return 0

    batches = (last - first) // BATCH
    lax.fori_loop(0, batches, some_rows, 0)
    for r in range(first + batches * BATCH, last):
        one_row(r)


def section_kernel(plan, section, place, q, numbers, *refs):
    refs = list(refs)
    size = plan.size
    early = [refs.pop(0) for _ in range(size)] if plan.early else []
    kept = refs.pop(0)
    first_one = section == plan.sections - 1
    halos = [refs.pop(0) for _ in range(2)] if first_one else []
    edges = [refs.pop(0) for _ in range(4)] if first_one else []
    q_win, n_win, buf_a, buf_b, coef, sems = refs
    members, window, lon = q_win.shape
    height = size * plan.tile
    base = place[section] * height
    start = pl.multiple_of(jnp.clip(base - 8, 0, plan.rows - window), 8)
    copies = [
        pltpu.make_async_copy(numbers.at[:, pl.ds(start, window), :], n_win, sems.at[0]),
        pltpu.make_async_copy(q.at[:, pl.ds(start, window), :], q_win, sems.at[1]),
    ]
    for i, first in enumerate((0, plan.rows - 8)) if first_one else []:
        rows = pl.ds(first, 8)
        copies.append(pltpu.make_async_copy(q.at[:, rows, :], edges[2 * i], sems.at[2 + 2 * i]))
        copies.append(
            pltpu.make_async_copy(numbers.at[:, rows, :], edges[2 * i + 1], sems.at[3 + 2 * i])
        )
    for copy in copies:
        copy.start()
    copies[0].wait()
    for i, c in enumerate(coefficients([n_win[i] for i in range(3)])):
        coef[i, 8 : 8 + window, :] = c
    copies[1].wait()
    shift = base - 8 - start

    def turn(g):
        at = pl.multiple_of(jnp.clip(g * 8 + shift, 0, window - 8), 8)
        return jnp.swapaxes(q_win[:, pl.ds(at, 8), :], 0, 1)

    def some_turns(g, _):
        buf_a[pl.ds(g * 8 - 4, 8)] = turn(g)
        return 0

    groups = height // 8 + 2
    buf_a[0:4] = turn(0)[4:]
    lax.fori_loop(1, groups - 1, some_turns, 0)
    buf_a[height + 4 : height + 8] = turn(groups - 1)[:4]
    src, dst = buf_a, buf_b
    for s in range(STEPS):
        step_rows(src, dst, coef, s + 1, height + 7 - s, shift + 12)
        src, dst = dst, src
    for i in range(size):
        r = section * size + i
        first = STEPS + (place[section] * size ^ r ^ place[plan.sections]) % size * plan.tile
        for slot, row in enumerate(plan.early):
            early[i][slot] = src[first + row]
        for slot, row in enumerate(plan.late):
            kept[i, slot] = src[first + row]
    for copy in copies[2:]:
        copy.wait()
    for side in range(2) if first_one else []:
        first = 0 if side == 0 else 8 - STEPS
        fields, stencil = edges[2 * side : 2 * side + 2]
        turned = jnp.swapaxes(fields[...], 0, 1)
        for row in range(STEPS):
            halos[side][row, :members] = turned[first + row]
            halos[side][row, members:] = jnp.zeros_like(halos[side][row, members:])
            for i in range(3):
                halos[side][row, members + i : members + i + 1] = stencil[
                    i, first + row : first + row + 1
                ]


def border_kernel(plan, place, low, high, q, numbers, *refs):
    kept = refs[: plan.sections]
    late = refs[plan.sections : plan.sections + plan.count]
    q_edge, n_edge, buf_a, buf_b, coef, final, sems = refs[plan.sections + plan.count :]
    me = place[plan.sections]
    members = q_edge.shape[1]
    wide = 3 * STEPS
    copies = []
    for side, first in enumerate((0, plan.rows - 2 * STEPS)):
        rows = pl.ds(first, 2 * STEPS)
        copies += [
            pltpu.make_async_copy(q.at[:, rows, :], q_edge.at[side], sems.at[2 * side]),
            pltpu.make_async_copy(numbers.at[:, rows, :], n_edge.at[side], sems.at[2 * side + 1]),
        ]
    for copy in copies:
        copy.start()
    for section in range(plan.sections):
        final[section * plan.size : (section + 1) * plan.size] = kept[section][...]
    for copy in copies:
        copy.wait()
    for side, halo in enumerate((low, high)):
        halo_at, own_at = (0, STEPS) if side == 0 else (2 * STEPS, 0)
        buf_a[halo_at : halo_at + STEPS] = halo[:, :members, :]
        buf_a[own_at : own_at + 2 * STEPS] = jnp.swapaxes(q_edge[side], 0, 1)
        halo_numbers = [halo[:, members + i, :] for i in range(3)]
        own_numbers = [n_edge[side, i] for i in range(3)]
        for i, (h, o) in enumerate(zip(coefficients(halo_numbers), coefficients(own_numbers))):
            coef[i, halo_at : halo_at + STEPS, :] = h
            coef[i, own_at : own_at + 2 * STEPS, :] = o
        src, dst = buf_a, buf_b
        for s in range(STEPS):
            step_rows(src, dst, coef, s + 1, wide - s - 1, 0)
            src, dst = dst, src
        for r in range(STEPS):
            row = r if side == 0 else plan.rows - STEPS + r
            final[me ^ (row // plan.tile), plan.late.index(row % plan.tile)] = src[STEPS + r]
    for r in range(plan.count):
        late[r][...] = final[r]


def split(x):
    high = x.astype(bf16)
    return high, (x - high.astype(f32)).astype(bf16)


def mm(a, b, dims=((1,), (0,))):
    return lax.dot_general(a, b, (dims, ((), ())), preferred_element_type=f32)


def analysis_kernel(plan, arrived, fresh, old_mix, old_fields, out_rows, keep_fields, *refs):
    refs = list(refs)
    count = plan.count
    take = lambda n: [refs.pop(0) for _ in range(n)]
    place, fresh_of, out_of = take(3)
    me = place[plan.sections]
    pieces = take(count) if arrived else []
    inn, prec, cells = take(3) if fresh else (None, None, None)
    weights = take(1)[0] if out_rows else None
    old_mix_refs = take(len(old_mix))
    old_field_refs = take(len(old_fields))
    mix_out = take(1)[0] if fresh else None
    kept_out = take(1)[0] if keep_fields else None
    outs = take(count) if out_rows else []
    mix, fields = take(2)
    tile = plan.tile
    members, lon = fields.shape[1:]
    share = members // count
    group = LANES // OB
    pack = plan.pack
    per_row = lon // LANES
    pairs = per_row // pack
    for slots, ref in zip(old_mix, old_mix_refs):
        for row, slot in slots:
            mix[row + 1] = ref[slot]
    for slots, ref in zip(old_fields, old_field_refs):
        for row, slot in slots:
            fields[row] = ref[slot]
    if arrived:
        for r in range(count):
            first = pl.multiple_of((me ^ r) * share, share)
            for slot, row in enumerate(arrived):
                fields[row, pl.ds(first, share), :] = pieces[r][slot]
    if fresh:

        def observe(slot, _):
            row = fresh_of[slot]
            for q in range(per_row // group):
                anomalies = []
                for t in range(group):
                    lanes = slice((q * group + t) * LANES, (q * group + t + 1) * LANES)
                    block = fields[row, :, lanes]
                    anomalies.append(block - jnp.mean(block, axis=0, keepdims=True))
                high, low = split(jnp.concatenate(anomalies, axis=0))
                at = row * (per_row // group) + q
                cell_row = cells[pl.ds(at, 1), :]
                chosen = (
                    lax.broadcasted_iota(jnp.int32, (LANES, LANES), 0)
                    == jnp.broadcast_to(cell_row, (LANES, LANES))
                )
                pick = jnp.where(chosen, 1.0, 0.0).astype(bf16)
                seen = mm(high, pick) + mm(low, pick)
                shape = seen.shape
                same = (
                    lax.broadcasted_iota(jnp.int32, shape, 0) // members
                    == lax.broadcasted_iota(jnp.int32, shape, 1) // OB
                )
                seen_high, seen_low = split(jnp.where(same, seen, 0.0))
                lanes = pl.ds(pl.multiple_of(at * LANES, LANES), LANES)
                weighted = inn[:, lanes] * prec[:, lanes]
                w_high, w_low = split(weighted)
                both = mm(
                    jnp.concatenate([w_high, w_low], axis=0), seen_high, ((1,), (1,))
                )
                total = both[:members] + both[members:] + mm(w_high, seen_low, ((1,), (1,)))
                wide = pack * members
                for k in range(group // pack):
                    mix[row + 1, q * (group // pack) + k] = total[:, k * wide : (k + 1) * wide]
            return 0

        lax.fori_loop(0, len(fresh), observe, 0)
        for slot, row in enumerate(fresh):
            mix_out[slot] = mix[row + 1]
    for slot, row in enumerate(keep_fields):
        kept_out[slot] = fields[row]
    if out_rows:
        reach = ceil_div(R, pack)
        width = 2 * reach + 1

        def update(slot, _):
            row = out_of[slot]
            for pair in range(pairs):
                sums = [jnp.zeros((members, pack * members), f32) for _ in range(pack)]
                for d in range(width):
                    place = pair + d - reach
                    step = place // pairs
                    part = mix[row + 1 + step, place - step * pairs]
                    for t in range(pack):
                        block = row * per_row + pair * pack + t
                        w = weights[block, pl.ds(d, 1), :]
                        sums[t] += part * jnp.broadcast_to(w, part.shape)
                for t in range(pack):
                    first = (pair * pack + t) * LANES
                    cells_here = fields[row, :, first : first + LANES]
                    anomaly = cells_here - jnp.mean(cells_here, axis=0, keepdims=True)
                    a_high, a_low = split(anomaly)
                    a_high = jnp.concatenate([a_high] * pack, axis=0)
                    a_low = jnp.concatenate([a_low] * pack, axis=0)
                    s_high, s_low = split(sums[t])
                    both = mm(jnp.concatenate([s_high, s_low], axis=0), a_high)
                    done = cells_here + both[:members] + both[members:] + mm(s_high, a_low)
                    fields[row, :, first : first + LANES] = done
            return 0

        lax.fori_loop(0, len(out_rows), update, 0)
        for r in range(count):
            first = pl.multiple_of((me ^ r) * share, share)
            for slot, row in enumerate(out_rows):
                outs[r][slot] = fields[row, pl.ds(first, share), :]


def assemble_kernel(plan, parts, place, *refs):
    pieces, (out, buf) = refs[:-2], refs[-2:]
    me = place[plan.sections]
    at = 0
    for rows in parts:
        for r in range(plan.count):
            base = (me ^ r) * plan.tile
            for slot, row in enumerate(rows):
                buf[base + row] = pieces[at + r][slot]
        at += plan.count

    def turn(g, _):
        r = pl.multiple_of(g * 8, 8)
        out[:, pl.ds(r, 8), :] = jnp.swapaxes(buf[pl.ds(r, 8)], 0, 1)
        return 0

    lax.fori_loop(0, plan.rows // 8, turn, 0)


class Plan:
    def __init__(self, rows, count, members, sections):
        assert count >= 4 and count & (count - 1) == 0
        self.rows = rows
        self.count = count
        self.sections = sections
        self.size = count // self.sections
        self.tile = rows // count
        self.pack = max(1, LANES // members)
        self.early = [r for r in range(self.tile) if STEPS <= r < self.tile - STEPS]
        self.late = [r for r in range(self.tile) if r not in self.early]


def shards(initial, stencil_numbers, innovations, obs_prec, obs_cell, band_idx):
    share, rows, lon = initial.shape
    count = lax.axis_size("member")
    members = share * count
    plan = Plan(rows, count, members, SECTIONS)
    tile, pack, size = plan.tile, plan.pack, plan.size
    per_row = lon // LANES
    pairs = per_row // pack
    me = lax.axis_index("member")
    place = jnp.stack([me // size ^ i for i in range(plan.sections)] + [me]).astype(jnp.int32)
    sds = lambda *shape: jax.ShapeDtypeStruct(shape, f32)
    ints = lambda values: jnp.array(list(values) or [0], jnp.int32)

    early_rows, late_rows = len(plan.early), len(plan.late)
    height = size * tile
    window = min(rows, height + (8 if plan.sections == 2 else 16))
    chain = Chain(FLIGHT)
    half = count // 2
    far, near = list(reversed(range(half, count))), list(reversed(range(1, half)))
    turns = far[:2]
    for i in range(half):
        turns += near[i : i + 1] + far[i + 2 : i + 3]

    def send(pieces, partners, *earlier):
        got = list(pieces)
        for r in partners:
            piece = after(pieces[r], *earlier) if earlier and r == partners[-1] else pieces[r]
            got[r] = chain.swap(piece, r)
        return got

    def forecast(section, order):
        shapes = []
        if plan.early:
            shapes = [sds(early_rows, share, lon)] * size
        shapes.append(sds(size, late_rows, share, lon))
        scratch = []
        if section == plan.sections - 1:
            shapes += [sds(STEPS, share + 8, lon)] * 2
            scratch = [pltpu.VMEM((share, 8, lon), f32), pltpu.VMEM((3, 8, lon), f32)] * 2
        return pl.pallas_call(
            functools.partial(section_kernel, plan, section),
            out_shape=shapes,
            in_specs=[SMEM, HBM, HBM],
            out_specs=[VMEM] * len(shapes),
            scratch_shapes=scratch
            + [
                pltpu.VMEM((share, window, lon), f32),
                pltpu.VMEM((3, window, lon), f32),
                pltpu.VMEM((height + 8, share, lon), f32),
                pltpu.VMEM((height + 8, share, lon), f32),
                pltpu.VMEM((5, window + 16, lon), f32),
                pltpu.SemaphoreType.DMA((6,)),
            ],
            compiler_params=params(SECTION_MIB),
            cost_estimate=hint(9),
            name=f"section_{section}",
        )(order, initial, stencil_numbers)

    order, early, kept = place, [], []
    for section in reversed(range(plan.sections)):
        outs = list(forecast(section, order))
        if section == plan.sections - 1:
            to_high, to_low = outs.pop(), outs.pop()
        kept.insert(0, outs.pop())
        early = outs + early
        order = after(place, kept[0])
    if plan.early:
        early = send(early, far[:2])
        low = chain.shift(to_high, "slab", 1)
        high = chain.shift(to_low, "slab", -1)
        early = send(early, far[2:3] + [r for r in turns[2:] if r != far[2]])
    else:
        low = chain.shift(to_high, "slab", 1)
        high = chain.shift(to_low, "slab", -1)
    late = pl.pallas_call(
        functools.partial(border_kernel, plan),
        out_shape=[sds(late_rows, share, lon)] * count,
        in_specs=[SMEM, VMEM, VMEM, HBM, HBM] + [VMEM] * plan.sections,
        out_specs=[VMEM] * count,
        scratch_shapes=[
            pltpu.VMEM((2, share, 2 * STEPS, lon), f32),
            pltpu.VMEM((2, 3, 2 * STEPS, lon), f32),
            pltpu.VMEM((3 * STEPS, share, lon), f32),
            pltpu.VMEM((3 * STEPS, share, lon), f32),
            pltpu.VMEM((5, 3 * STEPS, lon), f32),
            pltpu.VMEM((count, late_rows, share, lon), f32),
            pltpu.SemaphoreType.DMA((4,)),
        ],
        compiler_params=params(BORDER_MIB),
        cost_estimate=hint(4),
        name="border",
    )(place, low, high, initial, stencil_numbers, *kept)

    blocks = tile * per_row
    first_block = lax.axis_index(("slab", "member")) * blocks
    own = first_block + jnp.arange(blocks, dtype=jnp.int32)
    reach = ceil_div(R, pack)
    width = 2 * reach + 1
    start = own // pack * pack - reach * pack
    reached = start[:, None] + jnp.arange(width * pack, dtype=jnp.int32)
    in_band = jnp.any(reached[:, :, None] == band_idx[:, None, :], axis=2)
    distance = jnp.abs(reached - own[:, None]).astype(f32)
    tapers = jnp.where(in_band, 1.0 - distance / (R + 1.0), 0.0) / (members - 1)
    weights = jnp.repeat(tapers, members, axis=1).reshape(blocks, width, pack * members)
    prec = obs_prec.reshape(1, -1)
    cells = obs_cell.reshape(-1, LANES)

    def analyse(arrived, pieces, fresh, old_mix, old_fields, out_rows, keep_fields, name, order=place):
        args = [order, ints(fresh), ints(out_rows)]
        shapes = []
        if arrived:
            args += pieces
        if fresh:
            args += [innovations, prec, cells]
            shapes += [sds(len(fresh), pairs, members, pack * members)]
        if out_rows:
            args += [weights]
        args += [m[1] for m in old_mix] + [f[1] for f in old_fields]
        if keep_fields:
            shapes += [sds(len(keep_fields), members, lon)]
        if out_rows:
            shapes += [sds(len(out_rows), share, lon)] * count
        made = list(
            pl.pallas_call(
                functools.partial(
                    analysis_kernel,
                    plan,
                    arrived,
                    fresh,
                    [m[0] for m in old_mix],
                    [f[0] for f in old_fields],
                    out_rows,
                    keep_fields,
                ),
                out_shape=shapes,
                in_specs=[SMEM] * 3 + [VMEM] * (len(args) - 3),
                out_specs=[VMEM] * len(shapes),
                scratch_shapes=[
                    pltpu.VMEM((tile + 2, pairs, members, pack * members), f32),
                    pltpu.VMEM((tile, members, lon), f32),
                ],
                compiler_params=params(ANALYSIS_MIB),
                cost_estimate=hint(0 if name in SHORT else 1.2 * len(fresh)),
                name=name,
            )(*args)
        )
        mixing = made.pop(0) if fresh else None
        fields = made.pop(0) if keep_fields else None
        return mixing, fields, made

    order_b = near[:-1] + far + near[-1:]
    order_c = far + near
    order_d = turns
    slots = lambda rows: [(row, slot) for slot, row in enumerate(rows)]
    parts, returned = [], []
    inner = [r for r in plan.early if r - 1 in plan.early and r + 1 in plan.early]
    old_mix, old_fields, order = [], [], place
    if plan.early:
        edge = [r for r in plan.early if r not in inner]
        mixing, fields, back = analyse(
            plan.early, early, plan.early, [], [], inner, edge, "analyse_early"
        )
        old_mix = [(slots(plan.early), mixing)]
        old_fields = [(slots(edge), fields)] if edge else []
        late = send(late, order_b, fields if edge else mixing)
        order = after(place, mixing)
        if inner:
            parts.append(inner)
            back = send(back, order_c[:1])
    else:
        late = send(late, order_b)
    rims = sorted({0, tile - 1})
    rest = [r for r in plan.late if r not in rims]
    mixing, _, _ = analyse(plan.late, late, rims, [], [], [], [], "mix_rims", order)
    axes = ("slab", "member")
    from_prev = chain.shift(mixing[rims.index(tile - 1)][None], axes, 1)
    from_next = chain.shift(mixing[0][None], axes, -1)
    if inner:
        for r in order_c[1:]:
            back[r] = after(back[r], mixing)
        returned += send(back, order_c[1:])
    old_mix += [(slots(rims), mixing), ([(-1, 0)], from_prev), ([(tile, 0)], from_next)]
    if rest:
        mixing, _, _ = analyse(plan.late, late, rest, [], [], [], [], "mix_late", after(place, mixing))
        old_mix += [(slots(rest), mixing)]
    others = [r for r in range(tile) if r not in inner]
    _, _, back = analyse(plan.late, late, [], old_mix, old_fields, others, [], "analyse_late")
    parts.append(others)
    returned += send(back, order_d)

    return pl.pallas_call(
        functools.partial(assemble_kernel, plan, parts),
        out_shape=sds(share, rows, lon),
        in_specs=[SMEM] + [VMEM] * len(returned),
        out_specs=VMEM,
        scratch_shapes=[pltpu.VMEM((rows, share, lon), f32)],
        compiler_params=params(32),
        cost_estimate=hint(4),
        name="assemble",
    )(place, *returned)


def solution(mesh):
    in_specs = (
        P("member", "slab", None),
        P(None, "slab", None),
        P(None, ("slab", "member")),
        P(("slab", "member")),
        P(("slab", "member"), None),
        P(("slab", "member"), None),
    )
    out_specs = P("member", "slab", None)
    return jax.shard_map(shards, mesh=mesh, in_specs=in_specs, out_specs=out_specs, check_vma=False)
```
